32 devices in a mesh: groups: 2 (over y), img: 4 (over z), dsc: 2 (over x), rep: 2 (over core).
Axes of the slice: x: 2, y: 2, z: 4, core: 2. Of those that a mesh axis runs over, the one named last changes fastest.
Arguments:
- images: bfloat16 [2048, 2048], P(('groups', 'img'), 'dsc'), parts along dimension 0, may hold values from -6 to 6
- neighbours: int32 [2048, 10], P(('groups', 'img')), parts along dimension 0, may hold values from 0 to 1023, as said below
- similarity: float32 [2048, 10], P(('groups', 'img')), parts along dimension 0, may hold values from 0.3 to 1
- queries: bfloat16 [16384, 2048], P(('groups', 'rep'), 'dsc'), parts along dimension 0, may hold values from -6 to 6
- shortlist: int32 [16384, 2], P(('groups', 'rep')), parts along dimension 0, may hold values from 0 to 7, as said below
Outputs:
- augmented: bfloat16 [2048, 2048], P(('groups', 'img'), 'dsc'), parts along dimension 0
- scores: float32 [2, 8192, 256], P('rep', ('groups', 'img', 'dsc')), parts along dimension 1
The draws below stay inside these ranges and needn't reach their ends.
There are 2 independent parts, one for each index of `groups`. The reference program is written for one: setup_inputs(seed, part) draws one part's arguments, and reference() takes and returns one part's arrays. A program takes and returns all parts, laid end to end along the dimension named above; each array names one. Nothing has to cross between parts.
Inputs may be any that keep to these rules, and one draw needn't show every extreme that they name: `neighbours`: among the neighbour entries of the 128 rows of one aligned half of an image block, at most 640 name images of one image block of 256 ids (ids i * 256 to (i + 1) * 256 - 1); in every half some image block is named exactly 640 times, and both halves of an image block name the same image block that often. Split the queries into aligned groups of 512 (queries g * 512 to (g + 1) * 512 - 1). Among the 1024 shortlist entries of one group, at most 512 name blocks whose images lie in one image block of 256 ids; in every group some image block is named exactly 512 times.
All inputs are finite; a program needn't handle non-finite values.
Results may differ from the reference program's by a relative error of at most 0.0029.
Values may be sent and summed in bfloat16 or wider, within the bound.
A program may use at most 128 MiB of HBM per device.

```python
import jax
import jax.numpy as jnp
import numpy as np
from jax import lax

D = 2048
K = 10
BLK = 128
S = 2
IMG_DEV = 256
NQ_REP = 4096
HALF = 128
N_IMAGES = 1024
NQ = 8192
Q_DEV = 512
N_IMG = 4
N_REP = 2


def owner_order(block_key):
    return jax.random.permutation(block_key, N_IMG)


def entry_order(half_key):
    return jax.random.permutation(half_key, HALF * K)


def group_order(group_key):
    return jax.random.permutation(group_key, Q_DEV * S)


def owner_counts(entries, capacity):
    remainder = entries - capacity
    common = remainder // (N_IMG - 1)
    leftover = remainder % (N_IMG - 1)
    return [capacity] + [common + (1 if position < leftover else 0) for position in range(N_IMG - 1)]


def draw_neighbours(key, part):
    key = jax.random.fold_in(key, 11)
    entries = HALF * K
    capacity = 2 * entries // N_IMG
    counts = owner_counts(entries, capacity)
    rank_of = jnp.asarray(np.repeat(np.arange(N_IMG), counts), jnp.int32)
    block_keys = jax.random.split(jax.random.fold_in(key, 1), N_IMG)
    orders = jax.vmap(owner_order)(block_keys)
    owners = orders[:, rank_of]
    owners = jnp.stack([owners, owners], axis=1).reshape(2 * N_IMG, entries)
    half_keys = jax.random.split(jax.random.fold_in(key, 2), 2 * N_IMG)
    shuffles = jax.vmap(entry_order)(half_keys)
    owners = jnp.take_along_axis(owners, shuffles, axis=1)
    local_rows = jax.random.randint(jax.random.fold_in(key, 3), (2 * N_IMG, entries), 0, IMG_DEV)
    identity = owners * IMG_DEV + local_rows
    return identity.reshape(N_IMAGES, K).astype(jnp.int32)


def draw_shortlist(key, part):
    key = jax.random.fold_in(key, 13)
    entries = Q_DEV * S
    capacity = max(2, 2 * entries // N_IMG)
    group_count = NQ // Q_DEV
    counts = owner_counts(entries, capacity)
    rank_of = jnp.asarray(np.repeat(np.arange(N_IMG), counts), jnp.int32)
    group_keys = jax.random.split(jax.random.fold_in(key, 1), group_count)
    orders = jax.vmap(owner_order)(group_keys)
    owners = orders[:, rank_of]
    shuffle_keys = jax.random.split(jax.random.fold_in(key, 2), group_count)
    shuffles = jax.vmap(group_order)(shuffle_keys)
    owners = jnp.take_along_axis(owners, shuffles, axis=1)
    blocks_per = IMG_DEV // BLK
    local_blocks = jax.random.randint(jax.random.fold_in(key, 3), (group_count, entries), 0, blocks_per)
    identity = owners * blocks_per + local_blocks
    return identity.reshape(NQ, S).astype(jnp.int32)


def level_of(own_key, extent, cuts, smallest, high):
    def one(dim, parts):
        heights = jax.random.uniform(jax.random.fold_in(jax.random.fold_in(own_key, 6), dim), (parts,), jnp.float32, smallest / len(cuts), high / len(cuts))
        return jnp.repeat(jnp.exp(heights), extent[dim] // parts).reshape((-1,) + (1,) * (len(extent) - dim - 1))

    factor_of = one(*cuts[0])
    for cut in cuts[1:]:
        factor_of = factor_of * one(*cut)
    return factor_of


def normal_values(own_key, extent, width, limit, shards=(), held_as=jnp.bfloat16):
    level = level_of(own_key, extent, shards, -0.22, 0.18) if shards else 1.0
    drawn = jax.random.normal(own_key, extent, jnp.float32) * width * level
    return jnp.minimum(jnp.maximum(drawn, -limit), limit).astype(held_as)


def setup_inputs(seed: int = 0, part: int = 0) -> dict:
    arg_keys = jax.random.split(jax.random.key(seed), 6)
    part_keys = jax.random.split(jax.random.fold_in(arg_keys[5], part), 6)
    images = normal_values(part_keys[0], (N_IMAGES, D), 1.0, 6.0, ((0, 4), (1, 2)))
    neighbours = draw_neighbours(jax.random.fold_in(jax.random.fold_in(arg_keys[5], part), 71), part)
    similarity = jnp.clip(0.3 + 0.7 * jax.random.uniform(part_keys[2], (N_IMAGES, K), jnp.float32) ** level_of(part_keys[2], (N_IMAGES, K), ((0, 4),), -0.2, 0.2), 0.3, 1.0)
    queries = normal_values(part_keys[3], (NQ, D), 1.0, 6.0, ((0, 2), (1, 2)))
    shortlist = draw_shortlist(jax.random.fold_in(jax.random.fold_in(arg_keys[5], part), 71), part)
    return {"images": images, "neighbours": neighbours, "similarity": similarity, "queries": queries, "shortlist": shortlist}


epsilon = 1e-06

def reference(images, neighbours, similarity, queries, shortlist):
    weights = similarity ** 3
    summed = images.astype(jnp.float32)
    for column in range(K):
        summed = summed + weights[:, column:column + 1] * images[neighbours[:, column]].astype(jnp.float32)
    squares = lax.optimization_barrier(jnp.sum(summed * summed, axis=1, keepdims=True))
    augmented = (summed * lax.rsqrt(squares + epsilon)).astype(jnp.bfloat16)
    block_rows = 64 if NQ % 64 == 0 else NQ
    offsets = jnp.arange(BLK, dtype=jnp.int32)
    query_blocks = queries.reshape(NQ // block_rows, block_rows, D)
    list_blocks = shortlist.reshape(NQ // block_rows, block_rows, S)

    def score_block(pair):
        query_part, list_part = pair
        row_ids = (list_part[:, :, None] * BLK + offsets[None, None, :]).reshape(block_rows, S * BLK)
        chosen = augmented[row_ids].astype(jnp.float32)
        return jnp.einsum('qd,qcd->qc', query_part.astype(jnp.float32), chosen, precision=lax.Precision.HIGHEST)
    scores = lax.map(score_block, (query_blocks, list_blocks))
    return (augmented, scores.reshape(N_REP, NQ_REP, S * BLK))
```

```python
import functools

import jax
import jax.numpy as jnp
from jax import lax
from jax.experimental import pallas as pl
from jax.experimental.pallas import tpu as pltpu
from jax.sharding import PartitionSpec as P

BLK = 128
MESH = pl.DeviceIdType.MESH
epsilon = 1e-06


def each(count, body):
    if count <= 4:
        for index in range(count):
            body(index)
    else:

        def step(index, carry):
            body(index)
            return carry

        lax.fori_loop(0, count, step, 0)


def kernel(
    n_img, n_dsc, n_near, n_chunk, n_part, stored,
    img_ref, meta_ref, list_ref, q_hbm,
    aug_out, score_out,
    gath, metas, wt, acc, augt, sqs, qv, send_buf, recv_buf,
    q_sem, meta_send, meta_recv, z_right, z_left, z_recv, sib_send, sib_recv,
    sq_send, sq_recv, part_send, part_recv,
):
    me = lax.axis_index("img")
    my_d = lax.axis_index("dsc")
    my_r = lax.axis_index("rep")
    sib = 1 - my_r
    rows = img_ref.shape[0]
    n_block, width = gath.shape[1], gath.shape[2]
    part_rows = qv.shape[1]

    barrier = pltpu.get_barrier_semaphore()
    for t in range(1, n_img):
        pl.semaphore_signal(
            barrier, inc=1, device_id={"img": lax.rem(me + t, n_img)}, device_id_type=MESH
        )
    for t in range(1, n_dsc):
        pl.semaphore_signal(
            barrier, inc=1, device_id={"dsc": lax.rem(my_d + t, n_dsc)}, device_id_type=MESH
        )
    pl.semaphore_signal(barrier, inc=1, device_id={"rep": sib}, device_id_type=MESH)

    q_copy = pltpu.make_async_copy(q_hbm.at[me], qv, q_sem)
    q_copy.start()
    metas[me] = meta_ref[...]
    for b in range(n_block):
        gath[me, b] = img_ref[:, b * width : (b + 1) * width].T
    pl.semaphore_wait(barrier, n_img + n_dsc - 1)

    def meta_copy(t):
        return pltpu.make_async_remote_copy(
            src_ref=metas.at[me], dst_ref=metas.at[me],
            send_sem=meta_send.at[t], recv_sem=meta_recv.at[me],
            device_id={"img": lax.rem(me + t, n_img)}, device_id_type=MESH,
        )

    def meta_wait(p):
        pltpu.make_async_remote_copy(
            src_ref=metas.at[p], dst_ref=metas.at[p],
            send_sem=meta_send.at[0], recv_sem=meta_recv.at[p],
            device_id={"rep": sib}, device_id_type=MESH,
        ).wait_recv()

    def z_copy(p, c, side):
        piece = gath.at[p, my_r * n_chunk + c]
        return pltpu.make_async_remote_copy(
            src_ref=piece, dst_ref=piece,
            send_sem=(z_right if side > 0 else z_left).at[p, c], recv_sem=z_recv.at[p, c],
            device_id={"img": me + side}, device_id_type=MESH,
        )

    def z_wait(p, c):
        piece = gath.at[p, my_r * n_chunk + c]
        pltpu.make_async_remote_copy(
            src_ref=piece, dst_ref=piece,
            send_sem=z_right.at[p, c], recv_sem=z_recv.at[p, c],
            device_id={"rep": sib}, device_id_type=MESH,
        ).wait_recv()

    def sib_copy(p, c):
        piece = gath.at[p, my_r * n_chunk + c]
        return pltpu.make_async_remote_copy(
            src_ref=piece, dst_ref=piece,
            send_sem=sib_send.at[p, c], recv_sem=sib_recv.at[p, c],
            device_id={"rep": sib}, device_id_type=MESH,
        )

    def sib_wait(p, c):
        piece = gath.at[p, sib * n_chunk + c]
        pltpu.make_async_remote_copy(
            src_ref=piece, dst_ref=piece,
            send_sem=sib_send.at[p, c], recv_sem=sib_recv.at[p, c],
            device_id={"rep": sib}, device_id_type=MESH,
        ).wait_recv()

    for t in range(1, n_img):
        meta_copy(t).start()
    has_right, has_left = me + 1 < n_img, me > 0
    for c in range(n_chunk):

        @pl.when(has_right)
        def _():
            z_copy(me, c, 1).start()

        @pl.when(has_left)
        def _():
            z_copy(me, c, -1).start()

    def event(t, c):
        @pl.when(me >= t)
        def _():
            z_wait(me - t, c)

            @pl.when(has_right)
            def _():
                z_copy(me - t, c, 1).start()

            sib_copy(me - t, c).start()

        @pl.when(me + t < n_img)
        def _():
            z_wait(me + t, c)

            @pl.when(has_left)
            def _():
                z_copy(me + t, c, -1).start()

            sib_copy(me + t, c).start()

    def build(target, source, put):
        sub = 64
        lane = lax.broadcasted_iota(jnp.int32, (sub, rows), 1) + target * rows
        line = lax.broadcasted_iota(jnp.int32, (sub, rows), 0) + source * rows
        for j in range(rows // sub):
            here = line + j * sub
            value = jnp.where(here == lane, 1.0, 0.0)
            ids = here.astype(jnp.float32)
            for k in range(n_near):
                weight = metas[target, k : k + 1, :]
                near = metas[target, n_near + k : n_near + k + 1, :]
                value = value + jnp.where(near == ids, weight, 0.0)
            high = value.astype(jnp.bfloat16)
            low = (value - high.astype(jnp.float32)).astype(jnp.bfloat16)
            put(j * sub, sub, high, low)

    def build_target(target):
        @pl.loop(0, n_img)
        def _(source):
            def put(at, count, high, low):
                wt[source, target, at : at + count] = high
                wt[source, target, rows + at : rows + at + count] = low

            build(target, source, put)

    def spread(p, b, first):
        piece = gath[p, b]
        twice = jnp.concatenate([piece, piece], axis=1)
        for s in range(n_img):
            got = jnp.dot(twice, wt[p, s], preferred_element_type=jnp.float32)
            if first:
                acc[s, b] = got
            else:
                acc[s, b] = acc[s, b] + got

    def spread_slot(p):
        for c in range(n_chunk):
            spread(p, my_r * n_chunk + c, False)
            sib_wait(p, c)
            spread(p, sib * n_chunk + c, False)

    def spread_own():
        @pl.loop(0, n_block)
        def _(b):
            spread(me, b, True)

    def spread_step(t):
        @pl.when(me >= t)
        def _():
            spread_slot(me - t)

        @pl.when(me + t < n_img)
        def _():
            spread_slot(me + t)

    if stored:
        build_target(me)

        def build_step(t):
            p = lax.rem(me + t, n_img)
            meta_wait(p)
            build_target(p)

        pending = [functools.partial(build_step, t) for t in range(1, n_img)]
        ready = [spread_own]
        for t in range(1, n_img):
            for c in range(n_chunk):
                event(t, c)
                if pending:
                    pending.pop(0)()
                else:
                    for job in ready:
                        job()
                    ready = []
            ready.append(functools.partial(spread_step, t))
        for job in pending + ready:
            job()
    else:
        for t in range(1, n_img):
            meta_wait(lax.rem(me + t, n_img))
            for c in range(n_chunk):
                event(t, c)
        for t in range(1, n_img):
            for c in range(n_chunk):

                @pl.when(me >= t)
                def _():
                    sib_wait(me - t, c)

                @pl.when(me + t < n_img)
                def _():
                    sib_wait(me + t, c)

        acc[...] = jnp.zeros_like(acc)

        @pl.loop(0, n_img)
        def _(source):
            @pl.loop(0, n_img)
            def _(target):
                def put(at, count, high, low):
                    wt[0, 0, at : at + count] = high
                    wt[0, 0, rows + at : rows + at + count] = low

                build(target, source, put)

                @pl.loop(0, n_block)
                def _(b):
                    piece = gath[source, b]
                    twice = jnp.concatenate([piece, piece], axis=1)
                    acc[target, b] = acc[target, b] + jnp.dot(
                        twice, wt[0, 0], preferred_element_type=jnp.float32
                    )

    def squares(s):
        total = jnp.zeros((1, rows), jnp.float32)
        for b in range(n_block):
            value = acc[s, b]
            total = total + jnp.sum(value * value, axis=0, keepdims=True)
        sqs[my_d, s] = total

    each(n_img, squares)

    def sq_copy(t):
        return pltpu.make_async_remote_copy(
            src_ref=sqs.at[my_d], dst_ref=sqs.at[my_d],
            send_sem=sq_send.at[t], recv_sem=sq_recv.at[my_d],
            device_id={"dsc": lax.rem(my_d + t, n_dsc)}, device_id_type=MESH,
        )

    for t in range(1, n_dsc):
        sq_copy(t).start()
    q_copy.wait()
    for t in range(1, n_dsc):
        p = lax.rem(my_d + t, n_dsc)
        pltpu.make_async_remote_copy(
            src_ref=sqs.at[p], dst_ref=sqs.at[p],
            send_sem=sq_send.at[t], recv_sem=sq_recv.at[p],
            device_id={"rep": sib}, device_id_type=MESH,
        ).wait_recv()

    def normalise(s):
        total = sqs[0, s]
        for d in range(1, n_dsc):
            total = total + sqs[d, s]
        scale = lax.rsqrt(total + epsilon)
        for b in range(n_block):
            augt[s, b * width : (b + 1) * width, :] = (acc[s, b] * scale).astype(jnp.bfloat16)

    each(n_img, normalise)

    def score(at):
        query = qv[at]
        listed = list_ref[at]
        chosen = [jnp.zeros((part_rows, BLK), jnp.float32) for _ in range(listed.shape[1])]
        for s in range(n_img):
            dense = jnp.dot(query, augt[s], preferred_element_type=jnp.float32)
            for u in range(rows // BLK):
                one = dense[:, u * BLK : (u + 1) * BLK]
                block = s * (rows // BLK) + u
                for column in range(len(chosen)):
                    chosen[column] = jnp.where(
                        listed[:, column : column + 1] == block, one, chosen[column]
                    )
        return jnp.concatenate(chosen, axis=1)

    def part_copy(t, part):
        p = lax.rem(my_d + t, n_dsc)
        return pltpu.make_async_remote_copy(
            src_ref=send_buf.at[p, part], dst_ref=recv_buf.at[my_d, part],
            send_sem=part_send.at[p, part], recv_sem=part_recv.at[my_d, part],
            device_id={"dsc": p}, device_id_type=MESH,
        )

    for t in range(1, n_dsc):
        p = lax.rem(my_d + t, n_dsc)
        for part in range(n_part):
            send_buf[p, part] = score(p * n_part + part).astype(jnp.bfloat16)
            part_copy(t, part).start()

    for part in range(n_part):
        score_out[part] = score(my_d * n_part + part)
    for b in range(n_block):
        aug_out[:, b * width : (b + 1) * width] = augt[me, b * width : (b + 1) * width, :].T

    for part in range(n_part):
        total = score_out[part]
        for t in range(1, n_dsc):
            p = lax.rem(my_d + t, n_dsc)
            pltpu.make_async_remote_copy(
                src_ref=send_buf.at[p, part], dst_ref=recv_buf.at[p, part],
                send_sem=part_send.at[p, part], recv_sem=part_recv.at[p, part],
                device_id={"dsc": p}, device_id_type=MESH,
            ).wait_recv()
            total = total + recv_buf[p, part].astype(jnp.float32)
        score_out[part] = total

    for t in range(1, n_img):
        meta_copy(t).wait_send()
    if not stored or n_img < 2:
        pass
    for t in range(1, n_dsc):
        sq_copy(t).wait_send()
        for part in range(n_part):
            part_copy(t, part).wait_send()
    for c in range(n_chunk):

        @pl.when(has_right)
        def _():
            z_copy(me, c, 1).wait_send()

        @pl.when(has_left)
        def _():
            z_copy(me, c, -1).wait_send()

        for t in range(1, n_img):

            @pl.when(me >= t)
            def _():
                @pl.when(has_right)
                def _():
                    z_copy(me - t, c, 1).wait_send()

                sib_copy(me - t, c).wait_send()

            @pl.when(me + t < n_img)
            def _():
                @pl.when(has_left)
                def _():
                    z_copy(me + t, c, -1).wait_send()

                sib_copy(me + t, c).wait_send()


def per_device(images, neighbours, similarity, queries, shortlist):
    n_img, n_dsc = lax.axis_size("img"), lax.axis_size("dsc")
    rows, columns = images.shape
    n_near = neighbours.shape[1]
    own = queries.shape[0] // (n_img * n_dsc)
    part_rows = min(own, 128)
    n_part = own // part_rows
    n_chunk = 2 if columns // 4 >= 128 else 1
    width = columns // (2 * n_chunk)
    n_block = 2 * n_chunk
    stored = n_img <= 4
    pad = -2 * n_near % 8
    meta = jnp.concatenate(
        [
            (similarity**3).T,
            neighbours.T.astype(jnp.float32),
            jnp.zeros((pad, rows), jnp.float32),
        ],
        axis=0,
    )
    listed = lax.dynamic_index_in_dim(
        shortlist.reshape(n_img, n_dsc * n_part, part_rows, shortlist.shape[1]),
        lax.axis_index("img"), 0, keepdims=False,
    )
    answers = shortlist.shape[1] * BLK
    n_wt = n_img if stored else 1
    dma = pltpu.SemaphoreType.DMA
    vmem = pl.BlockSpec(memory_space=pltpu.VMEM)
    augmented, scores = pl.pallas_call(
        functools.partial(kernel, n_img, n_dsc, n_near, n_chunk, n_part, stored),
        out_shape=(
            jax.ShapeDtypeStruct((rows, columns), jnp.bfloat16),
            jax.ShapeDtypeStruct((n_part, part_rows, answers), jnp.float32),
        ),
        in_specs=[vmem, vmem, vmem, pl.BlockSpec(memory_space=pl.ANY)],
        out_specs=(vmem, vmem),
        scratch_shapes=[
            pltpu.VMEM((n_img, n_block, width, rows), jnp.bfloat16),
            pltpu.VMEM((n_img,) + meta.shape, jnp.float32),
            pltpu.VMEM((n_wt, n_wt, 2 * rows, rows), jnp.bfloat16),
            pltpu.VMEM((n_img, n_block, width, rows), jnp.float32),
            pltpu.VMEM((n_img, columns, rows), jnp.bfloat16),
            pltpu.VMEM((n_dsc, n_img, 1, rows), jnp.float32),
            pltpu.VMEM((n_dsc * n_part, part_rows, columns), jnp.bfloat16),
            pltpu.VMEM((n_dsc, n_part, part_rows, answers), jnp.bfloat16),
            pltpu.VMEM((n_dsc, n_part, part_rows, answers), jnp.bfloat16),
            dma,
            dma((n_img,)),
            dma((n_img,)),
            dma((n_img, n_chunk)),
            dma((n_img, n_chunk)),
            dma((n_img, n_chunk)),
            dma((n_img, n_chunk)),
            dma((n_img, n_chunk)),
            dma((n_dsc,)),
            dma((n_dsc,)),
            dma((n_dsc, n_part)),
            dma((n_dsc, n_part)),
        ],
        compiler_params=pltpu.CompilerParams(
            collective_id=0, has_side_effects=True, vmem_limit_bytes=40 * 1024 * 1024
        ),
    )(
        images, meta, listed,
        queries.reshape(n_img, n_dsc * n_part, part_rows, columns),
    )
    return augmented, scores.reshape(1, own, answers)


def solution(mesh):
    placed = (
        P(("groups", "img"), "dsc"),
        P(("groups", "img"), None),
        P(("groups", "img"), None),
        P(("groups", "rep"), "dsc"),
        P(("groups", "rep"), None),
    )
    return jax.shard_map(
        per_device,
        mesh=mesh,
        in_specs=placed,
        out_specs=(P(("groups", "img"), "dsc"), P("rep", ("groups", "img", "dsc"), None)),
        check_vma=False,
    )
```

```python
import functools

import jax
import jax.numpy as jnp
from jax import lax
from jax.experimental import pallas as pl
from jax.experimental.pallas import tpu as pltpu
from jax.sharding import PartitionSpec as P

BLK = 128
MESH = pl.DeviceIdType.MESH
epsilon = 1e-06


def each(count, body):
    if count <= 4:
        for index in range(count):
            body(index)
    else:

        def step(index, carry):
            body(index)
            return carry

        lax.fori_loop(0, count, step, 0)


def kernel(
    n_img, n_dsc, n_near, n_chunk, n_part, stored,
    img_ref, meta_ref, list_ref, q_hbm,
    aug_out, score_out,
    listed, gath, metas, wt, acc, augt, sqs, qv, send_buf, recv_buf,
    q_sem, meta_send, meta_recv, z_right, z_left, z_recv, sib_send, sib_recv,
    sq_send, sq_recv, part_send, part_recv,
):
    me = lax.axis_index("img")
    my_d = lax.axis_index("dsc")
    my_r = lax.axis_index("rep")
    sib = 1 - my_r
    rows = img_ref.shape[0]
    n_block, width = gath.shape[1], gath.shape[2]
    part_rows = qv.shape[1]

    barrier = pltpu.get_barrier_semaphore()
    for t in range(1, n_img):
        pl.semaphore_signal(
            barrier, inc=1, device_id={"img": lax.rem(me + t, n_img)}, device_id_type=MESH
        )
    for t in range(1, n_dsc):
        pl.semaphore_signal(
            barrier, inc=1, device_id={"dsc": lax.rem(my_d + t, n_dsc)}, device_id_type=MESH
        )
    pl.semaphore_signal(barrier, inc=1, device_id={"rep": sib}, device_id_type=MESH)

    q_copy = pltpu.make_async_copy(q_hbm.at[me], qv, q_sem)
    q_copy.start()
    metas[me] = meta_ref[...]
    for b in range(n_block):
        gath[me, b] = img_ref[:, b * width : (b + 1) * width].T
    pl.semaphore_wait(barrier, n_img + n_dsc - 1)

    def meta_copy(t):
        return pltpu.make_async_remote_copy(
            src_ref=metas.at[me], dst_ref=metas.at[me],
            send_sem=meta_send.at[t], recv_sem=meta_recv.at[me],
            device_id={"img": lax.rem(me + t, n_img)}, device_id_type=MESH,
        )

    def meta_wait(p):
        pltpu.make_async_remote_copy(
            src_ref=metas.at[p], dst_ref=metas.at[p],
            send_sem=meta_send.at[0], recv_sem=meta_recv.at[p],
            device_id={"rep": sib}, device_id_type=MESH,
        ).wait_recv()

    def z_copy(p, c, side):
        piece = gath.at[p, my_r * n_chunk + c]
        return pltpu.make_async_remote_copy(
            src_ref=piece, dst_ref=piece,
            send_sem=(z_right if side > 0 else z_left).at[p, c], recv_sem=z_recv.at[p, c],
            device_id={"img": me + side}, device_id_type=MESH,
        )

    def z_wait(p, c):
        piece = gath.at[p, my_r * n_chunk + c]
        pltpu.make_async_remote_copy(
            src_ref=piece, dst_ref=piece,
            send_sem=z_right.at[p, c], recv_sem=z_recv.at[p, c],
            device_id={"rep": sib}, device_id_type=MESH,
        ).wait_recv()

    def sib_copy(p, c):
        piece = gath.at[p, my_r * n_chunk + c]
        return pltpu.make_async_remote_copy(
            src_ref=piece, dst_ref=piece,
            send_sem=sib_send.at[p, c], recv_sem=sib_recv.at[p, c],
            device_id={"rep": sib}, device_id_type=MESH,
        )

    def sib_wait(p, c):
        piece = gath.at[p, sib * n_chunk + c]
        pltpu.make_async_remote_copy(
            src_ref=piece, dst_ref=piece,
            send_sem=sib_send.at[p, c], recv_sem=sib_recv.at[p, c],
            device_id={"rep": sib}, device_id_type=MESH,
        ).wait_recv()

    for t in range(1, n_img):
        meta_copy(t).start()
    has_right, has_left = me + 1 < n_img, me > 0
    for c in range(n_chunk):

        @pl.when(has_right)
        def _():
            z_copy(me, c, 1).start()

        @pl.when(has_left)
        def _():
            z_copy(me, c, -1).start()

    def event(t, c):
        @pl.when(me >= t)
        def _():
            z_wait(me - t, c)

            @pl.when(has_right)
            def _():
                z_copy(me - t, c, 1).start()

            sib_copy(me - t, c).start()

        @pl.when(me + t < n_img)
        def _():
            z_wait(me + t, c)

            @pl.when(has_left)
            def _():
                z_copy(me + t, c, -1).start()

            sib_copy(me + t, c).start()

    def build(target, source, put):
        sub = 64
        lane = lax.broadcasted_iota(jnp.int32, (sub, rows), 1) + target * rows
        line = lax.broadcasted_iota(jnp.int32, (sub, rows), 0) + source * rows
        for j in range(rows // sub):
            here = line + j * sub
            value = jnp.where(here == lane, 1.0, 0.0)
            ids = here.astype(jnp.float32)
            for k in range(n_near):
                weight = metas[target, k : k + 1, :]
                near = metas[target, n_near + k : n_near + k + 1, :]
                value = value + jnp.where(near == ids, weight, 0.0)
            high = value.astype(jnp.bfloat16)
            low = (value - high.astype(jnp.float32)).astype(jnp.bfloat16)
            put(j * sub, sub, high, low)

    def build_target(target):
        @pl.loop(0, n_img)
        def _(source):
            def put(at, count, high, low):
                wt[source, target, at : at + count] = high
                wt[source, target, rows + at : rows + at + count] = low

            build(target, source, put)

    def spread(p, b, first):
        piece = gath[p, b]
        twice = jnp.concatenate([piece, piece], axis=1)
        for s in range(n_img):
            got = jnp.dot(twice, wt[p, s], preferred_element_type=jnp.float32)
            if first:
                acc[s, b] = got
            else:
                acc[s, b] = acc[s, b] + got

    def spread_slot(p, c):
        spread(p, my_r * n_chunk + c, False)
        sib_wait(p, c)
        spread(p, sib * n_chunk + c, False)

    def spread_own():
        @pl.loop(0, n_block)
        def _(b):
            spread(me, b, True)

    def spread_step(t, c):
        @pl.when(me >= t)
        def _():
            spread_slot(me - t, c)

        @pl.when(me + t < n_img)
        def _():
            spread_slot(me + t, c)

    def spread_list():
        for column in range(list_ref.shape[0]):
            for j in range(list_ref.shape[1] // 128):
                span = slice(j * 128, (j + 1) * 128)
                line = list_ref[column : column + 1, span].astype(jnp.float32)
                listed[column, span, :] = jnp.broadcast_to(line, (128, 128)).T

    spread_list()
    if stored:
        build_target(me)

        def build_step(t):
            p = lax.rem(me + t, n_img)
            meta_wait(p)
            build_target(p)

        pending = [functools.partial(build_step, t) for t in range(1, n_img)]
        ready = [spread_own]
        for t in range(1, n_img):
            for c in range(n_chunk):
                event(t, c)
                if pending:
                    pending.pop(0)()
                else:
                    for job in ready:
                        job()
                    ready = []
                ready.append(functools.partial(spread_step, t, c))
        for job in pending + ready:
            job()
    else:
        for t in range(1, n_img):
            meta_wait(lax.rem(me + t, n_img))
            for c in range(n_chunk):
                event(t, c)
        for t in range(1, n_img):
            for c in range(n_chunk):

                @pl.when(me >= t)
                def _():
                    sib_wait(me - t, c)

                @pl.when(me + t < n_img)
                def _():
                    sib_wait(me + t, c)

        acc[...] = jnp.zeros_like(acc)

        @pl.loop(0, n_img)
        def _(source):
            @pl.loop(0, n_img)
            def _(target):
                def put(at, count, high, low):
                    wt[0, 0, at : at + count] = high
                    wt[0, 0, rows + at : rows + at + count] = low

                build(target, source, put)

                @pl.loop(0, n_block)
                def _(b):
                    piece = gath[source, b]
                    twice = jnp.concatenate([piece, piece], axis=1)
                    acc[target, b] = acc[target, b] + jnp.dot(
                        twice, wt[0, 0], preferred_element_type=jnp.float32
                    )

    def squares(s):
        total = jnp.zeros((1, rows), jnp.float32)
        for b in range(n_block):
            value = acc[s, b]
            total = total + jnp.sum(value * value, axis=0, keepdims=True)
        sqs[my_d, s] = total

    each(n_img, squares)

    def sq_copy(t):
        return pltpu.make_async_remote_copy(
            src_ref=sqs.at[my_d], dst_ref=sqs.at[my_d],
            send_sem=sq_send.at[t], recv_sem=sq_recv.at[my_d],
            device_id={"dsc": lax.rem(my_d + t, n_dsc)}, device_id_type=MESH,
        )

    for t in range(1, n_dsc):
        sq_copy(t).start()
    q_copy.wait()
    for t in range(1, n_dsc):
        p = lax.rem(my_d + t, n_dsc)
        pltpu.make_async_remote_copy(
            src_ref=sqs.at[p], dst_ref=sqs.at[p],
            send_sem=sq_send.at[t], recv_sem=sq_recv.at[p],
            device_id={"rep": sib}, device_id_type=MESH,
        ).wait_recv()

    def normalise(s):
        total = sqs[0, s]
        for d in range(1, n_dsc):
            total = total + sqs[d, s]
        scale = lax.rsqrt(total + epsilon)
        for b in range(n_block):
            augt[s, b * width : (b + 1) * width, :] = (acc[s, b] * scale).astype(jnp.bfloat16)

    each(n_img, normalise)

    def score(at):
        query = qv[at]
        span = pl.ds(pl.multiple_of(at * part_rows, part_rows), part_rows)
        asked = [listed[column, span, :] for column in range(list_ref.shape[0])]
        chosen = [jnp.zeros((part_rows, BLK), jnp.float32) for _ in asked]
        for s in range(n_img):
            dense = jnp.dot(query, augt[s], preferred_element_type=jnp.float32)
            for u in range(rows // BLK):
                one = dense[:, u * BLK : (u + 1) * BLK]
                block = s * (rows // BLK) + u
                for column in range(len(chosen)):
                    chosen[column] = jnp.where(asked[column] == block, one, chosen[column])
        return jnp.concatenate(chosen, axis=1)

    def part_copy(t, part):
        p = lax.rem(my_d + t, n_dsc)
        return pltpu.make_async_remote_copy(
            src_ref=send_buf.at[p, part], dst_ref=recv_buf.at[my_d, part],
            send_sem=part_send.at[p, part], recv_sem=part_recv.at[my_d, part],
            device_id={"dsc": p}, device_id_type=MESH,
        )

    for t in range(1, n_dsc):
        p = lax.rem(my_d + t, n_dsc)
        for part in range(n_part):
            send_buf[p, part] = score(p * n_part + part).astype(jnp.bfloat16)
            part_copy(t, part).start()

    for part in range(n_part):
        score_out[part] = score(my_d * n_part + part)
    for b in range(n_block):
        aug_out[:, b * width : (b + 1) * width] = augt[me, b * width : (b + 1) * width, :].T

    for part in range(n_part):
        total = score_out[part]
        for t in range(1, n_dsc):
            p = lax.rem(my_d + t, n_dsc)
            pltpu.make_async_remote_copy(
                src_ref=send_buf.at[p, part], dst_ref=recv_buf.at[p, part],
                send_sem=part_send.at[p, part], recv_sem=part_recv.at[p, part],
                device_id={"dsc": p}, device_id_type=MESH,
            ).wait_recv()
            total = total + recv_buf[p, part].astype(jnp.float32)
        score_out[part] = total

    for t in range(1, n_img):
        meta_copy(t).wait_send()
    for t in range(1, n_dsc):
        sq_copy(t).wait_send()
        for part in range(n_part):
            part_copy(t, part).wait_send()
    for c in range(n_chunk):

        @pl.when(has_right)
        def _():
            z_copy(me, c, 1).wait_send()

        @pl.when(has_left)
        def _():
            z_copy(me, c, -1).wait_send()

        for t in range(1, n_img):

            @pl.when(me >= t)
            def _():
                @pl.when(has_right)
                def _():
                    z_copy(me - t, c, 1).wait_send()

                sib_copy(me - t, c).wait_send()

            @pl.when(me + t < n_img)
            def _():
                @pl.when(has_left)
                def _():
                    z_copy(me + t, c, -1).wait_send()

                sib_copy(me + t, c).wait_send()


def per_device(images, neighbours, similarity, queries, shortlist):
    n_img, n_dsc = lax.axis_size("img"), lax.axis_size("dsc")
    rows, columns = images.shape
    n_near = neighbours.shape[1]
    own = queries.shape[0] // (n_img * n_dsc)
    part_rows = min(own, 128)
    n_part = own // part_rows
    n_chunk = 2 if columns // 4 >= 128 else 1
    width = columns // (2 * n_chunk)
    n_block = 2 * n_chunk
    stored = n_img <= 4
    pad = -2 * n_near % 8
    meta = jnp.concatenate(
        [
            (similarity**3).T,
            neighbours.T.astype(jnp.float32),
            jnp.zeros((pad, rows), jnp.float32),
        ],
        axis=0,
    )
    listed = lax.dynamic_slice_in_dim(
        shortlist.T, lax.axis_index("img") * n_dsc * own, n_dsc * own, axis=1
    )
    answers = shortlist.shape[1] * BLK
    n_wt = n_img if stored else 1
    dma = pltpu.SemaphoreType.DMA
    vmem = pl.BlockSpec(memory_space=pltpu.VMEM)
    augmented, scores = pl.pallas_call(
        functools.partial(kernel, n_img, n_dsc, n_near, n_chunk, n_part, stored),
        out_shape=(
            jax.ShapeDtypeStruct((rows, columns), jnp.bfloat16),
            jax.ShapeDtypeStruct((n_part, part_rows, answers), jnp.float32),
        ),
        in_specs=[vmem, vmem, vmem, pl.BlockSpec(memory_space=pl.ANY)],
        out_specs=(vmem, vmem),
        scratch_shapes=[
            pltpu.VMEM(listed.shape + (BLK,), jnp.float32),
            pltpu.VMEM((n_img, n_block, width, rows), jnp.bfloat16),
            pltpu.VMEM((n_img,) + meta.shape, jnp.float32),
            pltpu.VMEM((n_wt, n_wt, 2 * rows, rows), jnp.bfloat16),
            pltpu.VMEM((n_img, n_block, width, rows), jnp.float32),
            pltpu.VMEM((n_img, columns, rows), jnp.bfloat16),
            pltpu.VMEM((n_dsc, n_img, 1, rows), jnp.float32),
            pltpu.VMEM((n_dsc * n_part, part_rows, columns), jnp.bfloat16),
            pltpu.VMEM((n_dsc, n_part, part_rows, answers), jnp.bfloat16),
            pltpu.VMEM((n_dsc, n_part, part_rows, answers), jnp.bfloat16),
            dma,
            dma((n_img,)),
            dma((n_img,)),
            dma((n_img, n_chunk)),
            dma((n_img, n_chunk)),
            dma((n_img, n_chunk)),
            dma((n_img, n_chunk)),
            dma((n_img, n_chunk)),
            dma((n_dsc,)),
            dma((n_dsc,)),
            dma((n_dsc, n_part)),
            dma((n_dsc, n_part)),
        ],
        compiler_params=pltpu.CompilerParams(
            collective_id=0, has_side_effects=True, vmem_limit_bytes=52 * 1024 * 1024
        ),
    )(
        images, meta, listed,
        queries.reshape(n_img, n_dsc * n_part, part_rows, columns),
    )
    return augmented, scores.reshape(1, own, answers)


def solution(mesh):
    placed = (
        P(("groups", "img"), "dsc"),
        P(("groups", "img"), None),
        P(("groups", "img"), None),
        P(("groups", "rep"), "dsc"),
        P(("groups", "rep"), None),
    )
    return jax.shard_map(
        per_device,
        mesh=mesh,
        in_specs=placed,
        out_specs=(P(("groups", "img"), "dsc"), P("rep", ("groups", "img", "dsc"), None)),
        check_vma=False,
    )
```

```python
import functools

import jax
import jax.numpy as jnp
from jax import lax
from jax.experimental import pallas as pl
from jax.experimental.pallas import tpu as pltpu
from jax.sharding import PartitionSpec as P

BLK = 128
MESH = pl.DeviceIdType.MESH
epsilon = 1e-06


def each(count, body):
    if count <= 4:
        for index in range(count):
            body(index)
    else:

        def step(index, carry):
            body(index)
            return carry

        lax.fori_loop(0, count, step, 0)


def kernel(
    n_img, n_dsc, n_near, n_chunk, n_part, stored,
    img_ref, meta_ref, list_ref, q_hbm,
    aug_out, score_out,
    listed, gath, metas, wt, acc, augt, sqs, qv, send_buf, recv_buf,
    q_sem, meta_send, meta_recv, z_right, z_left, z_recv, sib_send, sib_recv,
    sq_send, sq_recv, part_send, part_recv,
):
    me = lax.axis_index("img")
    my_d = lax.axis_index("dsc")
    my_r = lax.axis_index("rep")
    sib = 1 - my_r
    rows = img_ref.shape[0]
    n_block, width = gath.shape[1], gath.shape[2]
    part_rows = qv.shape[1]

    barrier = pltpu.get_barrier_semaphore()
    for t in range(1, n_img):
        pl.semaphore_signal(
            barrier, inc=1, device_id={"img": lax.rem(me + t, n_img)}, device_id_type=MESH
        )
    for t in range(1, n_dsc):
        pl.semaphore_signal(
            barrier, inc=1, device_id={"dsc": lax.rem(my_d + t, n_dsc)}, device_id_type=MESH
        )
    pl.semaphore_signal(barrier, inc=1, device_id={"rep": sib}, device_id_type=MESH)

    q_copy = pltpu.make_async_copy(q_hbm.at[me], qv, q_sem)
    q_copy.start()
    metas[me] = meta_ref[...]
    for b in range(n_block):
        gath[me, b] = img_ref[:, b * width : (b + 1) * width].T
    pl.semaphore_wait(barrier, n_img + n_dsc - 1)

    def meta_copy(t):
        return pltpu.make_async_remote_copy(
            src_ref=metas.at[me], dst_ref=metas.at[me],
            send_sem=meta_send.at[t], recv_sem=meta_recv.at[me],
            device_id={"img": lax.rem(me + t, n_img)}, device_id_type=MESH,
        )

    def meta_wait(p):
        pltpu.make_async_remote_copy(
            src_ref=metas.at[p], dst_ref=metas.at[p],
            send_sem=meta_send.at[0], recv_sem=meta_recv.at[p],
            device_id={"rep": sib}, device_id_type=MESH,
        ).wait_recv()

    def z_copy(p, c, side):
        piece = gath.at[p, my_r * n_chunk + c]
        return pltpu.make_async_remote_copy(
            src_ref=piece, dst_ref=piece,
            send_sem=(z_right if side > 0 else z_left).at[p, c], recv_sem=z_recv.at[p, c],
            device_id={"img": me + side}, device_id_type=MESH,
        )

    def z_wait(p, c):
        piece = gath.at[p, my_r * n_chunk + c]
        pltpu.make_async_remote_copy(
            src_ref=piece, dst_ref=piece,
            send_sem=z_right.at[p, c], recv_sem=z_recv.at[p, c],
            device_id={"rep": sib}, device_id_type=MESH,
        ).wait_recv()

    def sib_copy(p, c):
        piece = gath.at[p, my_r * n_chunk + c]
        return pltpu.make_async_remote_copy(
            src_ref=piece, dst_ref=piece,
            send_sem=sib_send.at[p, c], recv_sem=sib_recv.at[p, c],
            device_id={"rep": sib}, device_id_type=MESH,
        )

    def sib_wait(p, c):
        piece = gath.at[p, sib * n_chunk + c]
        pltpu.make_async_remote_copy(
            src_ref=piece, dst_ref=piece,
            send_sem=sib_send.at[p, c], recv_sem=sib_recv.at[p, c],
            device_id={"rep": sib}, device_id_type=MESH,
        ).wait_recv()

    for t in range(1, n_img):
        meta_copy(t).start()
    has_right, has_left = me + 1 < n_img, me > 0
    for c in range(n_chunk):

        @pl.when(has_right)
        def _():
            z_copy(me, c, 1).start()

        @pl.when(has_left)
        def _():
            z_copy(me, c, -1).start()

    def event(t, c):
        @pl.when(me >= t)
        def _():
            z_wait(me - t, c)

            @pl.when(has_right)
            def _():
                z_copy(me - t, c, 1).start()

            sib_copy(me - t, c).start()

        @pl.when(me + t < n_img)
        def _():
            z_wait(me + t, c)

            @pl.when(has_left)
            def _():
                z_copy(me + t, c, -1).start()

            sib_copy(me + t, c).start()

    def build(target, source, put):
        sub = 64
        lane = lax.broadcasted_iota(jnp.int32, (sub, rows), 1) + target * rows
        line = lax.broadcasted_iota(jnp.int32, (sub, rows), 0) + source * rows
        for j in range(rows // sub):
            here = line + j * sub
            value = jnp.where(here == lane, 1.0, 0.0)
            ids = here.astype(jnp.float32)
            for k in range(n_near):
                weight = metas[target, k : k + 1, :]
                near = metas[target, n_near + k : n_near + k + 1, :]
                value = value + jnp.where(near == ids, weight, 0.0)
            high = value.astype(jnp.bfloat16)
            low = (value - high.astype(jnp.float32)).astype(jnp.bfloat16)
            put(j * sub, sub, high, low)

    def build_target(target):
        @pl.loop(0, n_img)
        def _(source):
            def put(at, count, high, low):
                wt[source, target, at : at + count] = high
                wt[source, target, rows + at : rows + at + count] = low

            build(target, source, put)

    def spread(p, b, first):
        piece = gath[p, b]
        twice = jnp.concatenate([piece, piece], axis=1)
        for s in range(n_img):
            got = jnp.dot(twice, wt[p, s], preferred_element_type=jnp.float32)
            if first:
                acc[s, b] = got
            else:
                acc[s, b] = acc[s, b] + got

    def spread_slot(p, c):
        spread(p, my_r * n_chunk + c, False)
        sib_wait(p, c)
        spread(p, sib * n_chunk + c, False)

    def spread_own():
        @pl.loop(0, n_block)
        def _(b):
            spread(me, b, True)

    def spread_step(t, c):
        @pl.when(me >= t)
        def _():
            spread_slot(me - t, c)

        @pl.when(me + t < n_img)
        def _():
            spread_slot(me + t, c)

    def spread_list():
        for column in range(list_ref.shape[0]):
            for j in range(list_ref.shape[1] // 128):
                span = slice(j * 128, (j + 1) * 128)
                line = list_ref[column : column + 1, span].astype(jnp.float32)
                listed[column, span, :] = jnp.broadcast_to(line, (128, 128)).T

    spread_list()
    if stored:
        build_target(me)

        def build_step(t):
            p = lax.rem(me + t, n_img)
            meta_wait(p)
            build_target(p)

        pending = [functools.partial(build_step, t) for t in range(1, n_img)]
        ready = [spread_own]
        for t in range(1, n_img):
            for c in range(n_chunk):
                event(t, c)
                ready.append(functools.partial(spread_step, t, c))
                if pending:
                    pending.pop(0)()
                else:
                    for job in ready:
                        job()
                    ready = []
        for job in pending + ready:
            job()
    else:
        for t in range(1, n_img):
            meta_wait(lax.rem(me + t, n_img))
            for c in range(n_chunk):
                event(t, c)
        for t in range(1, n_img):
            for c in range(n_chunk):

                @pl.when(me >= t)
                def _():
                    sib_wait(me - t, c)

                @pl.when(me + t < n_img)
                def _():
                    sib_wait(me + t, c)

        acc[...] = jnp.zeros_like(acc)

        @pl.loop(0, n_img)
        def _(source):
            @pl.loop(0, n_img)
            def _(target):
                def put(at, count, high, low):
                    wt[0, 0, at : at + count] = high
                    wt[0, 0, rows + at : rows + at + count] = low

                build(target, source, put)

                @pl.loop(0, n_block)
                def _(b):
                    piece = gath[source, b]
                    twice = jnp.concatenate([piece, piece], axis=1)
                    acc[target, b] = acc[target, b] + jnp.dot(
                        twice, wt[0, 0], preferred_element_type=jnp.float32
                    )

    def squares(s):
        total = jnp.zeros((1, rows), jnp.float32)
        for b in range(n_block):
            value = acc[s, b]
            total = total + jnp.sum(value * value, axis=0, keepdims=True)
        sqs[my_d, s] = total

    each(n_img, squares)

    def sq_copy(t):
        return pltpu.make_async_remote_copy(
            src_ref=sqs.at[my_d], dst_ref=sqs.at[my_d],
            send_sem=sq_send.at[t], recv_sem=sq_recv.at[my_d],
            device_id={"dsc": lax.rem(my_d + t, n_dsc)}, device_id_type=MESH,
        )

    for t in range(1, n_dsc):
        sq_copy(t).start()
    q_copy.wait()
    for t in range(1, n_dsc):
        p = lax.rem(my_d + t, n_dsc)
        pltpu.make_async_remote_copy(
            src_ref=sqs.at[p], dst_ref=sqs.at[p],
            send_sem=sq_send.at[t], recv_sem=sq_recv.at[p],
            device_id={"rep": sib}, device_id_type=MESH,
        ).wait_recv()

    def normalise(s):
        total = sqs[0, s]
        for d in range(1, n_dsc):
            total = total + sqs[d, s]
        scale = lax.rsqrt(total + epsilon)
        for b in range(n_block):
            augt[s, b * width : (b + 1) * width, :] = (acc[s, b] * scale).astype(jnp.bfloat16)

    each(n_img, normalise)

    def score(at):
        query = qv[at]
        span = pl.ds(pl.multiple_of(at * part_rows, part_rows), part_rows)
        asked = [listed[column, span, :] for column in range(list_ref.shape[0])]
        chosen = [jnp.zeros((part_rows, BLK), jnp.float32) for _ in asked]
        for s in range(n_img):
            dense = jnp.dot(query, augt[s], preferred_element_type=jnp.float32)
            for u in range(rows // BLK):
                one = dense[:, u * BLK : (u + 1) * BLK]
                block = s * (rows // BLK) + u
                for column in range(len(chosen)):
                    chosen[column] = jnp.where(asked[column] == block, one, chosen[column])
        return jnp.concatenate(chosen, axis=1)

    def part_copy(t, part):
        p = lax.rem(my_d + t, n_dsc)
        return pltpu.make_async_remote_copy(
            src_ref=send_buf.at[p, part], dst_ref=recv_buf.at[my_d, part],
            send_sem=part_send.at[p, part], recv_sem=part_recv.at[my_d, part],
            device_id={"dsc": p}, device_id_type=MESH,
        )

    for t in range(1, n_dsc):
        p = lax.rem(my_d + t, n_dsc)
        for part in range(n_part):
            send_buf[p, part] = score(p * n_part + part).astype(jnp.bfloat16)
            part_copy(t, part).start()

    for part in range(n_part):
        score_out[part] = score(my_d * n_part + part)
    for b in range(n_block):
        aug_out[:, b * width : (b + 1) * width] = augt[me, b * width : (b + 1) * width, :].T

    for part in range(n_part):
        total = score_out[part]
        for t in range(1, n_dsc):
            p = lax.rem(my_d + t, n_dsc)
            pltpu.make_async_remote_copy(
                src_ref=send_buf.at[p, part], dst_ref=recv_buf.at[p, part],
                send_sem=part_send.at[p, part], recv_sem=part_recv.at[p, part],
                device_id={"dsc": p}, device_id_type=MESH,
            ).wait_recv()
            total = total + recv_buf[p, part].astype(jnp.float32)
        score_out[part] = total

    for t in range(1, n_img):
        meta_copy(t).wait_send()
    for t in range(1, n_dsc):
        sq_copy(t).wait_send()
        for part in range(n_part):
            part_copy(t, part).wait_send()
    for c in range(n_chunk):

        @pl.when(has_right)
        def _():
            z_copy(me, c, 1).wait_send()

        @pl.when(has_left)
        def _():
            z_copy(me, c, -1).wait_send()

        for t in range(1, n_img):

            @pl.when(me >= t)
            def _():
                @pl.when(has_right)
                def _():
                    z_copy(me - t, c, 1).wait_send()

                sib_copy(me - t, c).wait_send()

            @pl.when(me + t < n_img)
            def _():
                @pl.when(has_left)
                def _():
                    z_copy(me + t, c, -1).wait_send()

                sib_copy(me + t, c).wait_send()


def per_device(images, neighbours, similarity, queries, shortlist):
    n_img, n_dsc = lax.axis_size("img"), lax.axis_size("dsc")
    rows, columns = images.shape
    n_near = neighbours.shape[1]
    own = queries.shape[0] // (n_img * n_dsc)
    part_rows = min(own, 128)
    n_part = own // part_rows
    n_chunk = 2 if columns // 4 >= 128 else 1
    width = columns // (2 * n_chunk)
    n_block = 2 * n_chunk
    stored = n_img <= 4
    pad = -2 * n_near % 8
    meta = jnp.concatenate(
        [
            (similarity**3).T,
            neighbours.T.astype(jnp.float32),
            jnp.zeros((pad, rows), jnp.float32),
        ],
        axis=0,
    )
    listed = lax.dynamic_slice_in_dim(
        shortlist.T, lax.axis_index("img") * n_dsc * own, n_dsc * own, axis=1
    )
    answers = shortlist.shape[1] * BLK
    n_wt = n_img if stored else 1
    dma = pltpu.SemaphoreType.DMA
    vmem = pl.BlockSpec(memory_space=pltpu.VMEM)
    augmented, scores = pl.pallas_call(
        functools.partial(kernel, n_img, n_dsc, n_near, n_chunk, n_part, stored),
        out_shape=(
            jax.ShapeDtypeStruct((rows, columns), jnp.bfloat16),
            jax.ShapeDtypeStruct((n_part, part_rows, answers), jnp.float32),
        ),
        in_specs=[vmem, vmem, vmem, pl.BlockSpec(memory_space=pl.ANY)],
        out_specs=(vmem, vmem),
        scratch_shapes=[
            pltpu.VMEM(listed.shape + (BLK,), jnp.float32),
            pltpu.VMEM((n_img, n_block, width, rows), jnp.bfloat16),
            pltpu.VMEM((n_img,) + meta.shape, jnp.float32),
            pltpu.VMEM((n_wt, n_wt, 2 * rows, rows), jnp.bfloat16),
            pltpu.VMEM((n_img, n_block, width, rows), jnp.float32),
            pltpu.VMEM((n_img, columns, rows), jnp.bfloat16),
            pltpu.VMEM((n_dsc, n_img, 1, rows), jnp.float32),
            pltpu.VMEM((n_dsc * n_part, part_rows, columns), jnp.bfloat16),
            pltpu.VMEM((n_dsc, n_part, part_rows, answers), jnp.bfloat16),
            pltpu.VMEM((n_dsc, n_part, part_rows, answers), jnp.bfloat16),
            dma,
            dma((n_img,)),
            dma((n_img,)),
            dma((n_img, n_chunk)),
            dma((n_img, n_chunk)),
            dma((n_img, n_chunk)),
            dma((n_img, n_chunk)),
            dma((n_img, n_chunk)),
            dma((n_dsc,)),
            dma((n_dsc,)),
            dma((n_dsc, n_part)),
            dma((n_dsc, n_part)),
        ],
        compiler_params=pltpu.CompilerParams(
            collective_id=0, has_side_effects=True, vmem_limit_bytes=52 * 1024 * 1024
        ),
    )(
        images, meta, listed,
        queries.reshape(n_img, n_dsc * n_part, part_rows, columns),
    )
    return augmented, scores.reshape(1, own, answers)


def solution(mesh):
    placed = (
        P(("groups", "img"), "dsc"),
        P(("groups", "img"), None),
        P(("groups", "img"), None),
        P(("groups", "rep"), "dsc"),
        P(("groups", "rep"), None),
    )
    return jax.shard_map(
        per_device,
        mesh=mesh,
        in_specs=placed,
        out_specs=(P(("groups", "img"), "dsc"), P("rep", ("groups", "img", "dsc"), None)),
        check_vma=False,
    )
```
